256 devices in a mesh: space: 32 (over z, y), filt: 8 (over x, core).
Axes of the slice: x: 4, y: 4, z: 8, core: 2. Of those that a mesh axis runs over, the one named last changes fastest.
Arguments:
- volume: bfloat16 [64, 32, 32, 256], P('space'), may hold values from -6 to 6
- first_weight: bfloat16 [3, 3, 3, 256, 256], P(None, None, None, None, 'filt'), may hold values from -0.078125 to 0.078125
- second_weight: bfloat16 [3, 3, 3, 256, 256], replicated, may hold values from -0.078125 to 0.078125
- cotangent: bfloat16 [64, 32, 32, 256], P('space', 'filt'), may hold values from -0.0234375 to 0.0234375
Outputs:
- output: bfloat16 [64, 32, 32, 256], P('space', 'filt')
- grad_first: bfloat16 [3, 3, 3, 256, 256], P(None, None, None, None, 'filt')
- grad_second: bfloat16 [3, 3, 3, 256, 256], replicated
The draws below stay inside these ranges and needn't reach their ends.
All inputs are finite; a program needn't handle non-finite values.
Results may differ from the reference program's by a relative error of at most 0.0095.
Values may be sent and summed in bfloat16 or wider, within the bound.
No kernel may reach another device: no remote copies, remote signals or barrier semaphores. Data moves between devices by JAX's collectives and lax.ppermute only.
A program may use at most 128 MiB of HBM per device.

```python
import jax
import jax.numpy as jnp
from jax import lax

C = 256
WIDTH = 32
DEPTH = 64
HEIGHT = 32


def spiked(result, key, source, target, parts, factor):
    owner, partner = [(jnp.arange(result.shape[dim]) // (result.shape[dim] // parts)).reshape([-1 if axis == dim else 1 for axis in range(result.ndim)]) for dim in (source, target)]
    chosen = jax.random.permutation(key, parts)[partner]
    strong = (owner == chosen) | (owner == (partner + parts // 2) % parts)
    return jnp.where(strong, factor * result, result)


def level_of(own_key, dims, cuts, low, high):
    def one(dim, parts):
        draws = jax.random.uniform(jax.random.fold_in(jax.random.fold_in(own_key, 6), dim), (parts,), jnp.float32, low / len(cuts), high / len(cuts))
        return jnp.repeat(jnp.exp(draws), dims[dim] // parts).reshape((-1,) + (1,) * (len(dims) - dim - 1))

    loudness = one(*cuts[0])
    for cut in cuts[1:]:
        loudness = loudness * one(*cut)
    return loudness


def gaussian(own_key, dims, scale, bound, cuts=(), held_as=jnp.bfloat16):
    result = scale * jax.random.normal(own_key, dims, jnp.float32)
    if cuts:
        result = result * level_of(own_key, dims, cuts, -0.22, 0.18)
    return jnp.clip(result, -bound, bound).astype(held_as)


def bell_draw_with(stream_key, dims, width, limit, cuts, heavy, dtype=jnp.bfloat16):
    array = width * jax.random.normal(stream_key, dims, jnp.float32)
    if cuts:
        array = array * level_of(stream_key, dims, cuts, -0.22, 0.18)
    return jnp.clip(spiked(array, jax.random.fold_in(stream_key, 3), *heavy), -limit, limit).astype(dtype)


def setup_inputs(seed: int = 0) -> dict:
    keys = jax.random.split(jax.random.key(seed), 5)
    return {
        "volume": gaussian(keys[0], (DEPTH, HEIGHT, WIDTH, C), 1.0, 6.0, ((0, 32),)),
        "first_weight": gaussian(keys[1], (3, 3, 3, C, C), (27 * C) ** -0.5, 0.078125, ((4, 8),)),
        "second_weight": gaussian(keys[2], (3, 3, 3, C, C), (27 * C) ** -0.5, 0.078125),
        "cotangent": bell_draw_with(keys[3], (DEPTH, HEIGHT, WIDTH, C), (1.0 / (DEPTH * HEIGHT * WIDTH) ** 0.5), 0.0234375, ((0, 32), (1, 8)), (0, 3, 32, 2.75)),
    }


def convolve(padded, weight):
    span_depth = padded.shape[0] - 2
    span_height = padded.shape[1] - 2
    span_width = padded.shape[2] - 2
    summed = None
    for tap_d in range(3):
        for tap_h in range(3):
            for tap_w in range(3):
                window = padded[tap_d:tap_d + span_depth, tap_h:tap_h + span_height, tap_w:tap_w + span_width]
                window = window.reshape(-1, padded.shape[3])
                product = jnp.dot(window, weight[tap_d, tap_h, tap_w], preferred_element_type=jnp.float32)
                summed = product if summed is None else summed + product
    return summed.reshape(span_depth, span_height, span_width, weight.shape[4])

def weight_grad(padded, gradient):
    span_depth, span_height, span_width, outer = gradient.shape
    flat_grad = gradient.reshape(-1, outer)
    pieces = []
    for tap_d in range(3):
        for tap_h in range(3):
            for tap_w in range(3):
                window = padded[tap_d:tap_d + span_depth, tap_h:tap_h + span_height, tap_w:tap_w + span_width]
                window = window.reshape(-1, padded.shape[3])
                pieces.append(lax.dot_general(window, flat_grad, (((0,), (0,)), ((), ())), preferred_element_type=jnp.float32))
    return jnp.stack(pieces).reshape(3, 3, 3, padded.shape[3], outer)

def reverse_taps(weight):
    return jnp.transpose(weight[::-1, ::-1, ::-1], (0, 1, 2, 4, 3))

def pad_all(field):
    return jnp.pad(field, ((1, 1), (1, 1), (1, 1), (0, 0)))

def silu_slope(value):
    sigma = jax.nn.sigmoid(value)
    return sigma * (1.0 + value * (1.0 - sigma))

def reference(volume, first_weight, second_weight, cotangent):
    padded_in = pad_all(volume)
    first_pre = convolve(padded_in, first_weight)
    first_act = jax.nn.silu(first_pre).astype(jnp.bfloat16)
    padded_act = pad_all(first_act)
    second_pre = convolve(padded_act, second_weight)
    output = jax.nn.silu(second_pre).astype(jnp.bfloat16)
    second_grad = (cotangent.astype(jnp.float32) * silu_slope(second_pre)).astype(jnp.bfloat16)
    grad_second = weight_grad(padded_act, second_grad).astype(jnp.bfloat16)
    hidden_grad = convolve(pad_all(second_grad), reverse_taps(second_weight)).astype(jnp.bfloat16)
    first_grad = (hidden_grad.astype(jnp.float32) * silu_slope(first_pre)).astype(jnp.bfloat16)
    grad_first = weight_grad(padded_in, first_grad).astype(jnp.bfloat16)
    return (output, grad_first, grad_second)
```

```python
import jax
import jax.numpy as jnp
from jax import lax
from jax.experimental import pallas as pl
from jax.experimental.pallas import tpu as pltpu
from jax.sharding import PartitionSpec as P

F32 = jnp.float32
BF16 = jnp.bfloat16
PARAMS = pltpu.CompilerParams(vmem_limit_bytes=48 * 2**20)
VMEM = pl.BlockSpec(memory_space=pltpu.VMEM)
SMEM = pl.BlockSpec(memory_space=pltpu.SMEM)


def lanes(rows):
    return lax.broadcasted_iota(jnp.int32, (rows, 128), 1)


def columns(rows, width=128):
    return lax.broadcasted_iota(jnp.int32, (rows, width), 0) % 32


def spread_taps(planes, wide, acc, part, up, down):
    acc[...] = jnp.zeros_like(acc)
    for plane in range(2):
        for first in range(0, 9, 2):
            count = min(2, 9 - first)
            product = lax.dot_general(
                planes(plane),
                wide[first * 128 : (first + count) * 128, :],
                (((1,), (1,)), ((), ())),
                preferred_element_type=F32,
            )
            for group in range(first, first + count):
                tap_d, tap_h = group // 3, group % 3
                target = plane + 2 - tap_d
                start = (2 - tap_h) * 32
                acc[target, start : start + 1024, :] += product[
                    :, (group - first) * 128 : (group - first + 1) * 128
                ]
    rows = 128
    lane = lanes(rows)
    column = columns(rows)
    for chunk in range(1024 // rows):
        base = 32 + chunk * rows
        whole = jnp.zeros((rows, 128), F32)
        for target in range(4):
            left = jnp.where(column == 0, 0.0, acc[target, base - 1 : base - 1 + rows, :])
            here = acc[target, base : base + rows, :]
            right = jnp.where(column == 31, 0.0, acc[target, base + 1 : base + 1 + rows, :])
            picked = jnp.where(
                lane < 32, left, jnp.where(lane < 64, here, jnp.where(lane < 96, right, 0.0))
            )
            picked = picked + pltpu.roll(picked, 32, 1)
            picked = picked + pltpu.roll(picked, 64, 1)
            whole = jnp.where(lane // 32 == target, picked, whole)
        part[chunk * rows : (chunk + 1) * rows, :] = whole
    lane = lanes(512)
    low, high = part[0:512, :], part[512:1024, :]
    up[...] = jnp.where(lane < 64, pltpu.roll(low, 64, 1), high)
    down[...] = jnp.where(lane < 64, low, pltpu.roll(high, 64, 1))


def completed(slab, part, below, above):
    lane = lanes(512)
    low = part[0:512, :] + jnp.where(lane < 64, below[...], pltpu.roll(above[...], 64, 1))
    high = part[512:1024, :] + jnp.where(lane < 64, pltpu.roll(below[...], 64, 1), above[...])
    both = jnp.concatenate([low, high], axis=0)
    lane = lanes(1024)
    outside = ((slab == 0) & (lane < 32)) | ((slab == 31) & (lane >= 96))
    return both, outside


def tap_products(moving, fixed, store):
    column = columns(1024)
    blank = jnp.zeros((8, 128), F32)
    shifted = [
        jnp.where(column == 0, 0.0, jnp.concatenate([blank[:1], moving[:-1]], axis=0)),
        moving,
        jnp.where(column == 31, 0.0, jnp.concatenate([moving[1:], blank[:1]], axis=0)),
    ]
    rows = jnp.concatenate([jnp.transpose(one).astype(BF16) for one in shifted], axis=0)
    for tap_h in range(3):
        start = (2 - tap_h) * 32
        first = jnp.dot(rows, fixed[0, start : start + 1024, :], preferred_element_type=F32)
        second = jnp.dot(rows, fixed[1, start : start + 1024, :], preferred_element_type=F32)
        for tap_w in range(3):
            for tap_d in range(3):
                at = tap_w * 128 + tap_d * 32
                store(
                    tap_d, tap_h, tap_w, first[at : at + 32, :] + second[at + 32 : at + 64, :]
                )


def conv_one_kernel(volume, weight, part, up, down, wide, acc):
    wide[...] = jnp.zeros_like(wide)
    for group in range(9):
        wide[group * 128 : group * 128 + 96, :] = weight[group * 96 : (group + 1) * 96, :]
    spread_taps(lambda plane: volume[plane], wide, acc, part, up, down)


def activate_kernel(slab, part, below, above, act, slope, blocks):
    pre, outside = completed(slab[0], part, below, above)
    sigma = 1.0 / (1.0 + jnp.exp(-pre))
    value = jnp.where(outside, 0.0, pre * sigma).astype(BF16)
    act[...] = value
    slope[...] = jnp.where(outside, 0.0, sigma * (1.0 + pre * (1.0 - sigma)))
    blank = jnp.zeros((32, 128), BF16)
    for block in range(8):
        low, high = (4 * block - 1) * 32, (4 * block + 5) * 32
        blocks[block, 32 if block == 0 else 0 : 160 if block == 7 else 192, :] = act[
            max(low, 0) : min(high, 1024), :
        ]
    blocks[0, 0:32, :] = blank
    blocks[7, 160:192, :] = blank


def conv_two_kernel(blocks, weight, cotangent, output, grad, field, acc):
    for plane in range(4):
        field[plane] = jnp.concatenate(
            [blocks[source][:, plane * 32 : (plane + 1) * 32] for source in range(8)], axis=1
        )
    for tap_w in range(3):
        total = None
        for tap_d in range(3):
            for tap_h in range(3):
                window = jnp.concatenate(
                    [
                        field[tap_d, tap_h * 32 : tap_h * 32 + 128, :],
                        field[tap_d + 1, tap_h * 32 : tap_h * 32 + 128, :],
                    ],
                    axis=0,
                )
                product = jnp.dot(
                    window,
                    weight[(tap_d * 3 + tap_h) * 3 + tap_w],
                    preferred_element_type=F32,
                )
                total = product if total is None else total + product
        acc[tap_w, 8:264, :] = total
    column = columns(256, 256)
    pre = (
        jnp.where(column == 0, 0.0, acc[0, 7:263, :])
        + acc[1, 8:264, :]
        + jnp.where(column == 31, 0.0, acc[2, 9:265, :])
    )
    sigma = 1.0 / (1.0 + jnp.exp(-pre))
    output[...] = (pre * sigma).astype(BF16)
    slope = sigma * (1.0 + pre * (1.0 - sigma))
    grad[...] = (cotangent[...].astype(F32) * slope).astype(BF16)


def grad_two_kernel(act, blocks, result, fixed):
    fixed[:, 0:32, :] = jnp.zeros((2, 32, 256), BF16)
    fixed[:, 1056:1088, :] = jnp.zeros((2, 32, 256), BF16)
    for plane in range(2):
        for block in range(8):
            fixed[plane, 32 + block * 128 : 160 + block * 128, :] = blocks[
                block, plane * 128 : (plane + 1) * 128, :
            ]

    def store(tap_d, tap_h, tap_w, value):
        result[(tap_d * 3 + tap_h) * 3 + tap_w] = value.astype(BF16)

    tap_products(act[...].astype(F32), fixed, store)
    for spare in range(27, 32):
        result[spare] = jnp.zeros((32, 256), BF16)


def hidden_kernel(blocks, weight, part, up, down, wide, acc, planes):
    wide[...] = jnp.zeros_like(wide)
    for group in range(9):
        for tap_w in range(3):
            at = group * 128 + tap_w * 32
            wide[at : at + 32, :] = weight[(8 - group) * 3 + 2 - tap_w]
    for plane in range(2):
        for block in range(8):
            planes[plane, block * 128 : (block + 1) * 128, :] = blocks[
                block, plane * 128 : (plane + 1) * 128, :
            ]
    spread_taps(lambda plane: planes[plane], wide, acc, part, up, down)


def grad_one_kernel(slab, part, below, above, slope, volume, result, fixed):
    fixed[:, 0:32, :] = jnp.zeros((2, 32, 256), BF16)
    fixed[:, 1056:1088, :] = jnp.zeros((2, 32, 256), BF16)
    fixed[:, 32:1056, :] = volume[...]
    hidden, outside = completed(slab[0], part, below, above)
    hidden = hidden.astype(BF16).astype(F32)
    first = jnp.where(outside, 0.0, hidden * slope[...]).astype(BF16).astype(F32)

    def store(tap_d, tap_h, tap_w, value):
        result[((2 - tap_d) * 3 + 2 - tap_h) * 3 + 2 - tap_w] = value.astype(BF16)

    tap_products(first, fixed, store)
    for spare in range(27, 32):
        result[spare] = jnp.zeros((32, 256), BF16)


def shape(dims, dtype):
    return jax.ShapeDtypeStruct(dims, dtype)


def call(kernel, in_specs, outs, scratch, *operands):
    return pl.pallas_call(
        kernel,
        out_shape=outs,
        in_specs=in_specs,
        out_specs=[VMEM] * len(outs),
        scratch_shapes=scratch,
        compiler_params=PARAMS,
    )(*operands)


def neighbours(up, down):
    count = lax.axis_size("space")
    forward = [(i, i + 1) for i in range(count - 1)]
    backward = [(i + 1, i) for i in range(count - 1)]
    return lax.ppermute(up, "space", forward), lax.ppermute(down, "space", backward)


def gather(block, axis):
    count = lax.axis_size(axis)
    return lax.all_to_all(jnp.broadcast_to(block, (count,) + block.shape), axis, 0, 0)


def reduced(taps):
    pieces = lax.all_to_all(taps, "space", 0, 0)
    return jnp.sum(pieces.astype(F32), axis=0).astype(BF16)


def body(volume, first_weight, second_weight, cotangent):
    slab = lax.axis_index("space").astype(jnp.int32).reshape(1)
    place = lax.axis_index("filt")
    vol = volume.reshape(2, 1024, 256)
    weight_one = jnp.transpose(first_weight, (0, 1, 2, 4, 3)).reshape(864, 256)
    weight_two = second_weight.reshape(27, 256, 256)
    own_two = lax.dynamic_slice_in_dim(weight_two, place * 32, 32, axis=1)
    sent = [shape((1024, 128), F32), shape((512, 128), F32), shape((512, 128), F32)]
    spread_scratch = [pltpu.VMEM((1152, 256), BF16), pltpu.VMEM((4, 1088, 128), F32)]

    part, up, down = call(
        conv_one_kernel, [VMEM] * 2, sent, spread_scratch, vol, weight_one
    )
    below, above = neighbours(up, down)
    act, slope, blocks = call(
        activate_kernel,
        [SMEM] + [VMEM] * 3,
        [shape((1024, 128), BF16), shape((1024, 128), F32), shape((8, 192, 128), BF16)],
        [],
        slab,
        part,
        below,
        above,
    )
    blocks = lax.all_to_all(blocks, "filt", 0, 0)
    output, second_grad = call(
        conv_two_kernel,
        [VMEM] * 3,
        [shape((256, 256), BF16)] * 2,
        [pltpu.VMEM((4, 192, 256), BF16), pltpu.VMEM((3, 272, 256), F32)],
        blocks,
        weight_two,
        cotangent.reshape(256, 256),
    )
    grads = gather(second_grad, "filt")
    taps = shape((32, 32, 256), BF16)
    (taps_two,) = call(
        grad_two_kernel, [VMEM] * 2, [taps], [pltpu.VMEM((2, 1088, 256), BF16)], act, grads
    )
    part, up, down = call(
        hidden_kernel,
        [VMEM] * 2,
        sent,
        spread_scratch + [pltpu.VMEM((2, 1024, 256), BF16)],
        grads,
        own_two,
    )
    below, above = neighbours(up, down)
    (taps_one,) = call(
        grad_one_kernel,
        [SMEM] + [VMEM] * 5,
        [taps],
        [pltpu.VMEM((2, 1088, 256), BF16)],
        slab,
        part,
        below,
        above,
        slope,
        vol,
    )
    own_grad_two = gather(reduced(taps_two), "space")[:27]
    own_grad_one = gather(reduced(taps_one), "space")[:27]
    grad_two = lax.all_gather(own_grad_two, "filt", axis=1, tiled=True)
    grad_one = jnp.transpose(own_grad_one.reshape(3, 3, 3, 32, 256), (0, 1, 2, 4, 3))
    return (
        output.reshape(2, 4, 32, 256),
        grad_one,
        grad_two.reshape(3, 3, 3, 256, 256),
    )


def solution(mesh):
    in_specs = (
        P("space", None, None, None),
        P(None, None, None, None, "filt"),
        P(),
        P("space", "filt", None, None),
    )
    out_specs = (P("space", "filt", None, None), P(None, None, None, None, "filt"), P())
    return jax.shard_map(body, mesh=mesh, in_specs=in_specs, out_specs=out_specs, check_vma=False)
```

```python
import jax
import jax.numpy as jnp
from jax import lax
from jax.experimental import pallas as pl
from jax.experimental.pallas import tpu as pltpu
from jax.sharding import PartitionSpec as P

F32 = jnp.float32
BF16 = jnp.bfloat16
PARAMS = pltpu.CompilerParams(vmem_limit_bytes=20 * 2**20)
VMEM = pl.BlockSpec(memory_space=pltpu.VMEM)
SMEM = pl.BlockSpec(memory_space=pltpu.SMEM)


def lanes(rows):
    return lax.broadcasted_iota(jnp.int32, (rows, 128), 1)


def columns(rows, width=128):
    return lax.broadcasted_iota(jnp.int32, (rows, width), 0) % 32


def spread_taps(planes, wide, acc, part, up, down):
    acc[...] = jnp.zeros_like(acc)
    for plane in range(2):
        for first in range(0, 9, 2):
            count = min(2, 9 - first)
            product = lax.dot_general(
                planes(plane),
                wide[first * 128 : (first + count) * 128, :],
                (((1,), (1,)), ((), ())),
                preferred_element_type=F32,
            )
            for group in range(first, first + count):
                tap_d, tap_h = group // 3, group % 3
                target = plane + 2 - tap_d
                start = (2 - tap_h) * 32
                acc[target, start : start + 1024, :] += product[
                    :, (group - first) * 128 : (group - first + 1) * 128
                ]
    rows = 128
    lane = lanes(rows)
    column = columns(rows)
    for chunk in range(1024 // rows):
        base = 32 + chunk * rows
        whole = jnp.zeros((rows, 128), F32)
        for target in range(4):
            left = jnp.where(column == 0, 0.0, acc[target, base - 1 : base - 1 + rows, :])
            here = acc[target, base : base + rows, :]
            right = jnp.where(column == 31, 0.0, acc[target, base + 1 : base + 1 + rows, :])
            picked = jnp.where(
                lane < 32, left, jnp.where(lane < 64, here, jnp.where(lane < 96, right, 0.0))
            )
            picked = picked + pltpu.roll(picked, 32, 1)
            picked = picked + pltpu.roll(picked, 64, 1)
            whole = jnp.where(lane // 32 == target, picked, whole)
        part[chunk * rows : (chunk + 1) * rows, :] = whole
    lane = lanes(512)
    low, high = part[0:512, :], part[512:1024, :]
    up[...] = jnp.where(lane < 64, pltpu.roll(low, 64, 1), high).astype(BF16)
    down[...] = jnp.where(lane < 64, low, pltpu.roll(high, 64, 1)).astype(BF16)


def completed(slab, part, below, above):
    lane = lanes(512)
    lower, upper = below[...].astype(F32), above[...].astype(F32)
    low = part[0:512, :] + jnp.where(lane < 64, lower, pltpu.roll(upper, 64, 1))
    high = part[512:1024, :] + jnp.where(lane < 64, pltpu.roll(lower, 64, 1), upper)
    both = jnp.concatenate([low, high], axis=0)
    lane = lanes(1024)
    outside = ((slab == 0) & (lane < 32)) | ((slab == 31) & (lane >= 96))
    return both, outside


def tap_products(moving, fixed, store):
    column = columns(1024)
    blank = jnp.zeros((8, 128), F32)
    shifted = [
        jnp.where(column == 0, 0.0, jnp.concatenate([blank[:1], moving[:-1]], axis=0)),
        moving,
        jnp.where(column == 31, 0.0, jnp.concatenate([moving[1:], blank[:1]], axis=0)),
    ]
    rows = jnp.concatenate([jnp.transpose(one).astype(BF16) for one in shifted], axis=0)
    for tap_h in range(3):
        start = (2 - tap_h) * 32
        first = jnp.dot(rows, fixed[0, start : start + 1024, :], preferred_element_type=F32)
        second = jnp.dot(rows, fixed[1, start : start + 1024, :], preferred_element_type=F32)
        for tap_w in range(3):
            for tap_d in range(3):
                at = tap_w * 128 + tap_d * 32
                store(
                    tap_d, tap_h, tap_w, first[at : at + 32, :] + second[at + 32 : at + 64, :]
                )


def conv_one_kernel(volume, weight, part, up, down, wide, acc):
    wide[...] = jnp.zeros_like(wide)
    for group in range(9):
        wide[group * 128 : group * 128 + 96, :] = weight[group * 96 : (group + 1) * 96, :]
    spread_taps(lambda plane: volume[plane], wide, acc, part, up, down)


def activate_kernel(slab, part, below, above, act, slope, blocks):
    pre, outside = completed(slab[0], part, below, above)
    sigma = 1.0 / (1.0 + jnp.exp(-pre))
    value = jnp.where(outside, 0.0, pre * sigma).astype(BF16)
    act[...] = value
    slope[...] = jnp.where(outside, 0.0, sigma * (1.0 + pre * (1.0 - sigma)))
    blank = jnp.zeros((32, 128), BF16)
    for block in range(8):
        low, high = (4 * block - 1) * 32, (4 * block + 5) * 32
        blocks[block, 32 if block == 0 else 0 : 160 if block == 7 else 192, :] = act[
            max(low, 0) : min(high, 1024), :
        ]
    blocks[0, 0:32, :] = blank
    blocks[7, 160:192, :] = blank


def conv_two_kernel(blocks, weight, cotangent, output, grad, field, acc):
    for plane in range(4):
        field[plane] = jnp.concatenate(
            [blocks[source][:, plane * 32 : (plane + 1) * 32] for source in range(8)], axis=1
        )
    for tap_w in range(3):
        total = None
        for tap_d in range(3):
            for tap_h in range(3):
                window = jnp.concatenate(
                    [
                        field[tap_d, tap_h * 32 : tap_h * 32 + 128, :],
                        field[tap_d + 1, tap_h * 32 : tap_h * 32 + 128, :],
                    ],
                    axis=0,
                )
                product = jnp.dot(
                    window,
                    weight[(tap_d * 3 + tap_h) * 3 + tap_w],
                    preferred_element_type=F32,
                )
                total = product if total is None else total + product
        acc[tap_w, 8:264, :] = total
    column = columns(256, 256)
    pre = (
        jnp.where(column == 0, 0.0, acc[0, 7:263, :])
        + acc[1, 8:264, :]
        + jnp.where(column == 31, 0.0, acc[2, 9:265, :])
    )
    sigma = 1.0 / (1.0 + jnp.exp(-pre))
    output[...] = (pre * sigma).astype(BF16)
    slope = sigma * (1.0 + pre * (1.0 - sigma))
    grad[...] = (cotangent[...].astype(F32) * slope).astype(BF16)


def assemble(place, mine, other, fixed):
    fixed[:, 0:32, :] = jnp.zeros((2, 32, 256), BF16)
    fixed[:, 1056:1088, :] = jnp.zeros((2, 32, 256), BF16)
    chip, core = place // 2, place % 2
    for step in range(4):
        row = (chip + 4 - step) % 4 * 256
        for blocks, side in ((mine, core), (other, 1 - core)):
            start = pl.multiple_of(32 + row + side * 128, 32)
            for plane in range(2):
                fixed[plane, pl.ds(start, 128), :] = blocks[
                    step, plane * 128 : (plane + 1) * 128, :
                ]


def back_kernel(place, act, mine, other, weight, part, up, down, result, fixed, wide, acc):
    assemble(place[0], mine, other, fixed)
    wide[...] = jnp.zeros_like(wide)
    for group in range(9):
        for tap_w in range(3):
            at = group * 128 + tap_w * 32
            wide[at : at + 32, :] = weight[(8 - group) * 3 + 2 - tap_w]
    spread_taps(lambda plane: fixed[plane, 32:1056, :], wide, acc, part, up, down)

    def store(tap_d, tap_h, tap_w, value):
        result[(tap_d * 3 + tap_h) * 3 + tap_w] = value.astype(BF16)

    tap_products(act[...].astype(F32), fixed, store)
    for spare in range(27, 32):
        result[spare] = jnp.zeros((32, 256), BF16)


def total_of(pieces, start):
    total = pieces[0, start : start + 32, :].astype(F32)
    for source in range(1, 32):
        total = total + pieces[source, start : start + 32, :].astype(F32)
    return total.astype(BF16)


def grad_one_kernel(slab, part, below, above, slope, volume, pieces, result, fixed):
    fixed[:, 0:32, :] = jnp.zeros((2, 32, 256), BF16)
    fixed[:, 1056:1088, :] = jnp.zeros((2, 32, 256), BF16)
    fixed[:, 32:1056, :] = volume[...]
    hidden, outside = completed(slab[0], part, below, above)
    hidden = hidden.astype(BF16).astype(F32)
    first = jnp.where(outside, 0.0, hidden * slope[...]).astype(BF16).astype(F32)

    def store(tap_d, tap_h, tap_w, value):
        result[((2 - tap_d) * 3 + 2 - tap_h) * 3 + 2 - tap_w, 0:32, :] = value.astype(BF16)

    tap_products(first, fixed, store)
    for spare in range(27, 32):
        result[spare, 0:32, :] = jnp.zeros((32, 256), BF16)
    total = total_of(pieces, 0)
    for target in range(32):
        result[target, 32:64, :] = total


def last_kernel(pieces, copies, whole):
    total = total_of(pieces, 0)
    for target in range(32):
        copies[target] = total
    for tap in range(27):
        whole[tap] = pieces[tap, 32:64, :]


def shape(dims, dtype):
    return jax.ShapeDtypeStruct(dims, dtype)


def call(kernel, in_specs, outs, scratch, *operands):
    moved = sum(2 * one.size for one in (*operands, *outs))
    return pl.pallas_call(
        kernel,
        out_shape=outs,
        in_specs=in_specs,
        out_specs=[VMEM] * len(outs),
        scratch_shapes=scratch,
        compiler_params=PARAMS,
        cost_estimate=pl.CostEstimate(
            flops=10**9, bytes_accessed=moved, transcendentals=0
        ),
    )(*operands)


def neighbours(up, down):
    count = lax.axis_size("space")
    forward = [(i, i + 1) for i in range(count - 1)]
    backward = [(i + 1, i) for i in range(count - 1)]
    return lax.ppermute(up, "space", forward), lax.ppermute(down, "space", backward)


def swapped(block):
    return lax.ppermute(block, "filt", [(i, i ^ 1) for i in range(8)])


def along_chips(block):
    shifts = [[(i, (i + 2 * step) % 8) for i in range(8)] for step in (1, 2, 3)]
    return [block] + [lax.ppermute(block, "filt", shift) for shift in shifts]


def body(volume, first_weight, second_weight, cotangent):
    slab = lax.axis_index("space").astype(jnp.int32).reshape(1)
    place = lax.axis_index("filt").astype(jnp.int32)
    vol = volume.reshape(2, 1024, 256)
    weight_one = jnp.transpose(first_weight, (0, 1, 2, 4, 3)).reshape(864, 256)
    weight_two = second_weight.reshape(27, 256, 256)
    own_two = lax.dynamic_slice_in_dim(weight_two, place * 32, 32, axis=1)
    sent = [shape((1024, 128), F32)] + [shape((512, 128), BF16)] * 2
    spread_scratch = [pltpu.VMEM((1152, 256), BF16), pltpu.VMEM((4, 1088, 128), F32)]

    part, up, down = call(
        conv_one_kernel, [VMEM] * 2, sent, spread_scratch, vol, weight_one
    )
    below, above = neighbours(up, down)
    act, slope, blocks = call(
        activate_kernel,
        [SMEM] + [VMEM] * 3,
        [shape((1024, 128), BF16), shape((1024, 128), F32), shape((8, 192, 128), BF16)],
        [],
        slab,
        part,
        below,
        above,
    )
    blocks = lax.all_to_all(blocks, "filt", 0, 0)
    output, second_grad = call(
        conv_two_kernel,
        [VMEM] * 3,
        [shape((256, 256), BF16)] * 2,
        [pltpu.VMEM((4, 192, 256), BF16), pltpu.VMEM((3, 272, 256), F32)],
        blocks,
        weight_two,
        cotangent.reshape(256, 256),
    )
    mine = jnp.stack(along_chips(second_grad))
    other = swapped(mine)
    part, up, down, taps_two = call(
        back_kernel,
        [SMEM] + [VMEM] * 4,
        sent + [shape((32, 32, 256), BF16)],
        [pltpu.VMEM((2, 1088, 256), BF16)] + spread_scratch,
        place.reshape(1),
        act,
        mine,
        other,
        own_two,
    )
    below, above = neighbours(up, down)
    pieces = lax.all_to_all(taps_two, "space", 0, 0)
    (both,) = call(
        grad_one_kernel,
        [SMEM] + [VMEM] * 6,
        [shape((32, 64, 256), BF16)],
        [pltpu.VMEM((2, 1088, 256), BF16)],
        slab,
        part,
        below,
        above,
        slope,
        vol,
        pieces,
    )
    both = lax.all_to_all(both, "space", 0, 0)
    copies, own_grad_two = call(
        last_kernel,
        [VMEM],
        [shape((32, 32, 256), BF16), shape((27, 32, 256), BF16)],
        [],
        both,
    )
    grad_two = lax.all_gather(own_grad_two, "filt", axis=1, tiled=True)
    own_grad_one = lax.all_to_all(copies, "space", 0, 0)[:27]
    grad_one = jnp.transpose(own_grad_one.reshape(3, 3, 3, 32, 256), (0, 1, 2, 4, 3))
    return (
        output.reshape(2, 4, 32, 256),
        grad_one,
        grad_two.reshape(3, 3, 3, 256, 256),
    )


def solution(mesh):
    in_specs = (
        P("space", None, None, None),
        P(None, None, None, None, "filt"),
        P(),
        P("space", "filt", None, None),
    )
    out_specs = (P("space", "filt", None, None), P(None, None, None, None, "filt"), P())
    return jax.shard_map(body, mesh=mesh, in_specs=in_specs, out_specs=out_specs, check_vma=False)
```

```python
import jax
import jax.numpy as jnp
from jax import lax
from jax.experimental import pallas as pl
from jax.experimental.pallas import tpu as pltpu
from jax.sharding import PartitionSpec as P

F32 = jnp.float32
BF16 = jnp.bfloat16
PARAMS = pltpu.CompilerParams(vmem_limit_bytes=20 * 2**20)
VMEM = pl.BlockSpec(memory_space=pltpu.VMEM)
SMEM = pl.BlockSpec(memory_space=pltpu.SMEM)


def lanes(rows):
    return lax.broadcasted_iota(jnp.int32, (rows, 128), 1)


def columns(rows, width=128):
    return lax.broadcasted_iota(jnp.int32, (rows, width), 0) % 32


def spread_taps(planes, wide, acc, part, up, down):
    acc[...] = jnp.zeros_like(acc)
    for plane in range(2):
        for first in range(0, 9, 2):
            count = min(2, 9 - first)
            product = lax.dot_general(
                planes(plane),
                wide[first * 128 : (first + count) * 128, :],
                (((1,), (1,)), ((), ())),
                preferred_element_type=F32,
            )
            for group in range(first, first + count):
                tap_d, tap_h = group // 3, group % 3
                target = plane + 2 - tap_d
                start = (2 - tap_h) * 32
                acc[target, start : start + 1024, :] += product[
                    :, (group - first) * 128 : (group - first + 1) * 128
                ]
    rows = 128
    lane = lanes(rows)
    column = columns(rows)
    for chunk in range(1024 // rows):
        base = 32 + chunk * rows
        whole = jnp.zeros((rows, 128), F32)
        for target in range(4):
            left = jnp.where(column == 0, 0.0, acc[target, base - 1 : base - 1 + rows, :])
            here = acc[target, base : base + rows, :]
            right = jnp.where(column == 31, 0.0, acc[target, base + 1 : base + 1 + rows, :])
            picked = jnp.where(
                lane < 32, left, jnp.where(lane < 64, here, jnp.where(lane < 96, right, 0.0))
            )
            picked = picked + pltpu.roll(picked, 32, 1)
            picked = picked + pltpu.roll(picked, 64, 1)
            whole = jnp.where(lane // 32 == target, picked, whole)
        part[chunk * rows : (chunk + 1) * rows, :] = whole
    lane = lanes(512)
    low, high = part[0:512, :], part[512:1024, :]
    up[...] = jnp.where(lane < 64, pltpu.roll(low, 64, 1), high).astype(BF16)
    down[...] = jnp.where(lane < 64, low, pltpu.roll(high, 64, 1)).astype(BF16)


def completed(slab, part, below, above):
    lane = lanes(512)
    lower, upper = below[...].astype(F32), above[...].astype(F32)
    low = part[0:512, :] + jnp.where(lane < 64, lower, pltpu.roll(upper, 64, 1))
    high = part[512:1024, :] + jnp.where(lane < 64, pltpu.roll(lower, 64, 1), upper)
    both = jnp.concatenate([low, high], axis=0)
    lane = lanes(1024)
    outside = ((slab == 0) & (lane < 32)) | ((slab == 31) & (lane >= 96))
    return both, outside


def tap_products(moving, fixed, store):
    column = columns(1024)
    blank = jnp.zeros((8, 128), F32)
    shifted = [
        jnp.where(column == 0, 0.0, jnp.concatenate([blank[:1], moving[:-1]], axis=0)),
        moving,
        jnp.where(column == 31, 0.0, jnp.concatenate([moving[1:], blank[:1]], axis=0)),
    ]
    rows = jnp.concatenate([jnp.transpose(one).astype(BF16) for one in shifted], axis=0)
    for tap_h in range(3):
        start = (2 - tap_h) * 32
        first = jnp.dot(rows, fixed[0, start : start + 1024, :], preferred_element_type=F32)
        second = jnp.dot(rows, fixed[1, start : start + 1024, :], preferred_element_type=F32)
        for tap_w in range(3):
            for tap_d in range(3):
                at = tap_w * 128 + tap_d * 32
                store(
                    tap_d, tap_h, tap_w, first[at : at + 32, :] + second[at + 32 : at + 64, :]
                )


def conv_one_kernel(volume, weight, part, up, down, wide, acc):
    wide[...] = jnp.zeros_like(wide)
    for group in range(9):
        wide[group * 128 : group * 128 + 96, :] = weight[group * 96 : (group + 1) * 96, :]
    spread_taps(lambda plane: volume[plane], wide, acc, part, up, down)


def activate_kernel(slab, part, below, above, act, slope, blocks):
    pre, outside = completed(slab[0], part, below, above)
    sigma = 1.0 / (1.0 + jnp.exp(-pre))
    value = jnp.where(outside, 0.0, pre * sigma).astype(BF16)
    act[...] = value
    slope[...] = jnp.where(outside, 0.0, sigma * (1.0 + pre * (1.0 - sigma)))
    blank = jnp.zeros((32, 128), BF16)
    for block in range(8):
        low, high = (4 * block - 1) * 32, (4 * block + 5) * 32
        blocks[block, 32 if block == 0 else 0 : 160 if block == 7 else 192, :] = act[
            max(low, 0) : min(high, 1024), :
        ]
    blocks[0, 0:32, :] = blank
    blocks[7, 160:192, :] = blank


def conv_two_kernel(blocks, weight, cotangent, output, grad, field, acc):
    for plane in range(4):
        field[plane] = jnp.concatenate(
            [blocks[source][:, plane * 32 : (plane + 1) * 32] for source in range(8)], axis=1
        )
    for tap_w in range(3):
        total = None
        for tap_d in range(3):
            for tap_h in range(3):
                window = jnp.concatenate(
                    [
                        field[tap_d, tap_h * 32 : tap_h * 32 + 128, :],
                        field[tap_d + 1, tap_h * 32 : tap_h * 32 + 128, :],
                    ],
                    axis=0,
                )
                product = jnp.dot(
                    window,
                    weight[(tap_d * 3 + tap_h) * 3 + tap_w],
                    preferred_element_type=F32,
                )
                total = product if total is None else total + product
        acc[tap_w, 8:264, :] = total
    column = columns(256, 256)
    pre = (
        jnp.where(column == 0, 0.0, acc[0, 7:263, :])
        + acc[1, 8:264, :]
        + jnp.where(column == 31, 0.0, acc[2, 9:265, :])
    )
    sigma = 1.0 / (1.0 + jnp.exp(-pre))
    output[...] = (pre * sigma).astype(BF16)
    slope = sigma * (1.0 + pre * (1.0 - sigma))
    grad[...] = (cotangent[...].astype(F32) * slope).astype(BF16)


def assemble(place, mine, other, fixed):
    fixed[:, 0:32, :] = jnp.zeros((2, 32, 256), BF16)
    fixed[:, 1056:1088, :] = jnp.zeros((2, 32, 256), BF16)
    chip, core = place // 2, place % 2
    for step in range(4):
        row = (chip + 4 - step) % 4 * 256
        for blocks, side in ((mine, core), (other, 1 - core)):
            start = pl.multiple_of(32 + row + side * 128, 32)
            for plane in range(2):
                fixed[plane, pl.ds(start, 128), :] = blocks[
                    step, plane * 128 : (plane + 1) * 128, :
                ]


def back_kernel(place, act, mine, other, weight, part, up, down, result, fixed, wide, acc):
    assemble(place[0], mine, other, fixed)
    wide[...] = jnp.zeros_like(wide)
    for group in range(9):
        for tap_w in range(3):
            at = group * 128 + tap_w * 32
            wide[at : at + 32, :] = weight[(8 - group) * 3 + 2 - tap_w]
    spread_taps(lambda plane: fixed[plane, 32:1056, :], wide, acc, part, up, down)

    def store(tap_d, tap_h, tap_w, value):
        result[(tap_d * 3 + tap_h) * 3 + tap_w] = value.astype(BF16)

    tap_products(act[...].astype(F32), fixed, store)
    for spare in range(27, 32):
        result[spare] = jnp.zeros((32, 256), BF16)


def total_of(pieces, start):
    total = pieces[0, start : start + 32, :].astype(F32)
    for source in range(1, 32):
        total = total + pieces[source, start : start + 32, :].astype(F32)
    return total.astype(BF16)


def grad_one_kernel(slab, part, below, above, slope, volume, pieces, result, fixed):
    fixed[:, 0:32, :] = jnp.zeros((2, 32, 256), BF16)
    fixed[:, 1056:1088, :] = jnp.zeros((2, 32, 256), BF16)
    fixed[:, 32:1056, :] = volume[...]
    hidden, outside = completed(slab[0], part, below, above)
    hidden = hidden.astype(BF16).astype(F32)
    first = jnp.where(outside, 0.0, hidden * slope[...]).astype(BF16).astype(F32)

    def store(tap_d, tap_h, tap_w, value):
        result[((2 - tap_d) * 3 + 2 - tap_h) * 3 + 2 - tap_w, 0:32, :] = value.astype(BF16)

    tap_products(first, fixed, store)
    for spare in range(27, 32):
        result[spare, 0:32, :] = jnp.zeros((32, 256), BF16)
    total = total_of(pieces, 0)
    for target in range(32):
        result[target, 32:64, :] = total


def last_kernel(pieces, copies, whole):
    total = total_of(pieces, 0)
    for target in range(32):
        copies[target] = total
    for tap in range(27):
        whole[tap] = pieces[tap, 32:64, :]


def join_kernel(place, *refs):
    chip, core = place[0] // 2, place[0] % 2
    whole = refs[8]
    for step in range(4):
        row = (chip + 4 - step) % 4 * 64
        for block, side in ((refs[step], core), (refs[4 + step], 1 - core)):
            start = pl.multiple_of(row + side * 32, 32)
            whole[:, pl.ds(start, 32), :] = block[...]


def join(place, blocks):
    piece = pl.BlockSpec((9, 32, 256), lambda step: (step, 0, 0))
    return pl.pallas_call(
        join_kernel,
        grid=(3,),
        cost_estimate=pl.CostEstimate(flops=2 * 10**9, bytes_accessed=0, transcendentals=0),
        out_shape=shape((27, 256, 256), BF16),
        in_specs=[SMEM] + [piece] * 8,
        out_specs=pl.BlockSpec((9, 256, 256), lambda step: (step, 0, 0)),
        compiler_params=PARAMS,
    )(place, *blocks)


def shape(dims, dtype):
    return jax.ShapeDtypeStruct(dims, dtype)


def call(kernel, in_specs, outs, scratch, *operands):
    return pl.pallas_call(
        kernel,
        out_shape=outs,
        in_specs=in_specs,
        out_specs=[VMEM] * len(outs),
        scratch_shapes=scratch,
        compiler_params=PARAMS,
    )(*operands)


def neighbours(up, down):
    count = lax.axis_size("space")
    forward = [(i, i + 1) for i in range(count - 1)]
    backward = [(i + 1, i) for i in range(count - 1)]
    return lax.ppermute(up, "space", forward), lax.ppermute(down, "space", backward)


def swapped(block):
    return lax.ppermute(block, "filt", [(i, i ^ 1) for i in range(8)])


def along_chips(block):
    shifts = [[(i, (i + 2 * step) % 8) for i in range(8)] for step in (1, 2, 3)]
    return [block] + [lax.ppermute(block, "filt", shift) for shift in shifts]


def body(volume, first_weight, second_weight, cotangent):
    slab = lax.axis_index("space").astype(jnp.int32).reshape(1)
    place = lax.axis_index("filt").astype(jnp.int32)
    vol = volume.reshape(2, 1024, 256)
    weight_one = jnp.transpose(first_weight, (0, 1, 2, 4, 3)).reshape(864, 256)
    weight_two = second_weight.reshape(27, 256, 256)
    own_two = lax.dynamic_slice_in_dim(weight_two, place * 32, 32, axis=1)
    sent = [shape((1024, 128), F32)] + [shape((512, 128), BF16)] * 2
    spread_scratch = [pltpu.VMEM((1152, 256), BF16), pltpu.VMEM((4, 1088, 128), F32)]

    part, up, down = call(
        conv_one_kernel, [VMEM] * 2, sent, spread_scratch, vol, weight_one
    )
    below, above = neighbours(up, down)
    act, slope, blocks = call(
        activate_kernel,
        [SMEM] + [VMEM] * 3,
        [shape((1024, 128), BF16), shape((1024, 128), F32), shape((8, 192, 128), BF16)],
        [],
        slab,
        part,
        below,
        above,
    )
    blocks = lax.all_to_all(blocks, "filt", 0, 0)
    output, second_grad = call(
        conv_two_kernel,
        [VMEM] * 3,
        [shape((256, 256), BF16)] * 2,
        [pltpu.VMEM((4, 192, 256), BF16), pltpu.VMEM((3, 272, 256), F32)],
        blocks,
        weight_two,
        cotangent.reshape(256, 256),
    )
    mine = jnp.stack(along_chips(second_grad))
    other = swapped(mine)
    part, up, down, taps_two = call(
        back_kernel,
        [SMEM] + [VMEM] * 4,
        sent + [shape((32, 32, 256), BF16)],
        [pltpu.VMEM((2, 1088, 256), BF16)] + spread_scratch,
        place.reshape(1),
        act,
        mine,
        other,
        own_two,
    )
    below, above = neighbours(up, down)
    pieces = lax.all_to_all(taps_two, "space", 0, 0)
    (both,) = call(
        grad_one_kernel,
        [SMEM] + [VMEM] * 6,
        [shape((32, 64, 256), BF16)],
        [pltpu.VMEM((2, 1088, 256), BF16)],
        slab,
        part,
        below,
        above,
        slope,
        vol,
        pieces,
    )
    both = lax.all_to_all(both, "space", 0, 0)
    copies, own_grad_two = call(
        last_kernel,
        [VMEM],
        [shape((32, 32, 256), BF16), shape((27, 32, 256), BF16)],
        [],
        both,
    )
    chips = along_chips(own_grad_two)
    grad_two = join(place.reshape(1), chips + [swapped(block) for block in chips])
    own_grad_one = lax.all_to_all(copies, "space", 0, 0)[:27]
    grad_one = jnp.transpose(own_grad_one.reshape(3, 3, 3, 32, 256), (0, 1, 2, 4, 3))
    return (
        output.reshape(2, 4, 32, 256),
        grad_one,
        grad_two.reshape(3, 3, 3, 256, 256),
    )


def solution(mesh):
    in_specs = (
        P("space", None, None, None),
        P(None, None, None, None, "filt"),
        P(),
        P("space", "filt", None, None),
    )
    out_specs = (P("space", "filt", None, None), P(None, None, None, None, "filt"), P())
    return jax.shard_map(body, mesh=mesh, in_specs=in_specs, out_specs=out_specs, check_vma=False)
```

```python
import jax
import jax.numpy as jnp
from jax import lax
from jax.experimental import pallas as pl
from jax.experimental.pallas import tpu as pltpu
from jax.sharding import PartitionSpec as P

F32 = jnp.float32
BF16 = jnp.bfloat16
PARAMS = pltpu.CompilerParams(vmem_limit_bytes=20 * 2**20)
VMEM = pl.BlockSpec(memory_space=pltpu.VMEM)
SMEM = pl.BlockSpec(memory_space=pltpu.SMEM)


def lanes(rows):
    return lax.broadcasted_iota(jnp.int32, (rows, 128), 1)


def columns(rows, width=128):
    return lax.broadcasted_iota(jnp.int32, (rows, width), 0) % 32


def spread_taps(planes, wide, acc, part, up, down):
    acc[...] = jnp.zeros_like(acc)
    for plane in range(2):
        for first in range(0, 9, 2):
            count = min(2, 9 - first)
            product = lax.dot_general(
                planes(plane),
                wide[first * 128 : (first + count) * 128, :],
                (((1,), (1,)), ((), ())),
                preferred_element_type=F32,
            )
            for group in range(first, first + count):
                tap_d, tap_h = group // 3, group % 3
                target = plane + 2 - tap_d
                start = (2 - tap_h) * 32
                acc[target, start : start + 1024, :] += product[
                    :, (group - first) * 128 : (group - first + 1) * 128
                ]
    rows = 128
    lane = lanes(rows)
    column = columns(rows)
    for chunk in range(1024 // rows):
        base = 32 + chunk * rows
        whole = jnp.zeros((rows, 128), F32)
        for target in range(4):
            left = jnp.where(column == 0, 0.0, acc[target, base - 1 : base - 1 + rows, :])
            here = acc[target, base : base + rows, :]
            right = jnp.where(column == 31, 0.0, acc[target, base + 1 : base + 1 + rows, :])
            picked = jnp.where(
                lane < 32, left, jnp.where(lane < 64, here, jnp.where(lane < 96, right, 0.0))
            )
            picked = picked + pltpu.roll(picked, 32, 1)
            picked = picked + pltpu.roll(picked, 64, 1)
            whole = jnp.where(lane // 32 == target, picked, whole)
        part[chunk * rows : (chunk + 1) * rows, :] = whole
    lane = lanes(512)
    low, high = part[0:512, :], part[512:1024, :]
    up[...] = jnp.where(lane < 64, pltpu.roll(low, 64, 1), high).astype(BF16)
    down[...] = jnp.where(lane < 64, low, pltpu.roll(high, 64, 1)).astype(BF16)


def completed(slab, part, below, above):
    lane = lanes(512)
    lower, upper = below[...].astype(F32), above[...].astype(F32)
    low = part[0:512, :] + jnp.where(lane < 64, lower, pltpu.roll(upper, 64, 1))
    high = part[512:1024, :] + jnp.where(lane < 64, pltpu.roll(lower, 64, 1), upper)
    both = jnp.concatenate([low, high], axis=0)
    lane = lanes(1024)
    outside = ((slab == 0) & (lane < 32)) | ((slab == 31) & (lane >= 96))
    return both, outside


def tap_products(moving, fixed, store):
    column = columns(1024)
    blank = jnp.zeros((8, 128), F32)
    shifted = [
        jnp.where(column == 0, 0.0, jnp.concatenate([blank[:1], moving[:-1]], axis=0)),
        moving,
        jnp.where(column == 31, 0.0, jnp.concatenate([moving[1:], blank[:1]], axis=0)),
    ]
    rows = jnp.concatenate([jnp.transpose(one).astype(BF16) for one in shifted], axis=0)
    for tap_h in range(3):
        start = (2 - tap_h) * 32
        first = jnp.dot(rows, fixed[0, start : start + 1024, :], preferred_element_type=F32)
        second = jnp.dot(rows, fixed[1, start : start + 1024, :], preferred_element_type=F32)
        for tap_w in range(3):
            for tap_d in range(3):
                at = tap_w * 128 + tap_d * 32
                store(
                    tap_d, tap_h, tap_w, first[at : at + 32, :] + second[at + 32 : at + 64, :]
                )


def conv_one_kernel(volume, weight, part, up, down, wide, acc):
    wide[...] = jnp.zeros_like(wide)
    for group in range(9):
        wide[group * 128 : group * 128 + 96, :] = weight[group * 96 : (group + 1) * 96, :]
    spread_taps(lambda plane: volume[plane], wide, acc, part, up, down)


def activate_kernel(slab, part, below, above, act, slope, blocks):
    pre, outside = completed(slab[0], part, below, above)
    sigma = 1.0 / (1.0 + jnp.exp(-pre))
    value = jnp.where(outside, 0.0, pre * sigma).astype(BF16)
    act[...] = value
    slope[...] = jnp.where(outside, 0.0, sigma * (1.0 + pre * (1.0 - sigma)))
    blank = jnp.zeros((32, 128), BF16)
    for block in range(8):
        low, high = (4 * block - 1) * 32, (4 * block + 5) * 32
        blocks[block, 32 if block == 0 else 0 : 160 if block == 7 else 192, :] = act[
            max(low, 0) : min(high, 1024), :
        ]
    blocks[0, 0:32, :] = blank
    blocks[7, 160:192, :] = blank


def conv_two_kernel(blocks, weight, cotangent, output, grad, field, acc):
    for plane in range(4):
        field[plane] = jnp.concatenate(
            [blocks[source][:, plane * 32 : (plane + 1) * 32] for source in range(8)], axis=1
        )
    for tap_w in range(3):
        total = None
        for tap_d in range(3):
            for tap_h in range(3):
                window = jnp.concatenate(
                    [
                        field[tap_d, tap_h * 32 : tap_h * 32 + 128, :],
                        field[tap_d + 1, tap_h * 32 : tap_h * 32 + 128, :],
                    ],
                    axis=0,
                )
                product = jnp.dot(
                    window,
                    weight[(tap_d * 3 + tap_h) * 3 + tap_w],
                    preferred_element_type=F32,
                )
                total = product if total is None else total + product
        acc[tap_w, 8:264, :] = total
    column = columns(256, 256)
    pre = (
        jnp.where(column == 0, 0.0, acc[0, 7:263, :])
        + acc[1, 8:264, :]
        + jnp.where(column == 31, 0.0, acc[2, 9:265, :])
    )
    sigma = 1.0 / (1.0 + jnp.exp(-pre))
    output[...] = (pre * sigma).astype(BF16)
    slope = sigma * (1.0 + pre * (1.0 - sigma))
    grad[...] = (cotangent[...].astype(F32) * slope).astype(BF16)


def assemble(place, mine, other, fixed):
    fixed[:, 0:32, :] = jnp.zeros((2, 32, 256), BF16)
    fixed[:, 1056:1088, :] = jnp.zeros((2, 32, 256), BF16)
    chip, core = place // 2, place % 2
    for step in range(4):
        row = (chip + 4 - step) % 4 * 256
        for blocks, side in ((mine, core), (other, 1 - core)):
            start = pl.multiple_of(32 + row + side * 128, 32)
            for plane in range(2):
                fixed[plane, pl.ds(start, 128), :] = blocks[
                    step, plane * 128 : (plane + 1) * 128, :
                ]


def back_kernel(place, act, mine, other, weight, part, up, down, result, fixed, wide, acc):
    assemble(place[0], mine, other, fixed)
    wide[...] = jnp.zeros_like(wide)
    for group in range(9):
        for tap_w in range(3):
            at = group * 128 + tap_w * 32
            wide[at : at + 32, :] = weight[(8 - group) * 3 + 2 - tap_w]
    spread_taps(lambda plane: fixed[plane, 32:1056, :], wide, acc, part, up, down)

    def store(tap_d, tap_h, tap_w, value):
        result[(tap_d * 3 + tap_h) * 3 + tap_w] = value.astype(BF16)

    tap_products(act[...].astype(F32), fixed, store)
    for spare in range(27, 32):
        result[spare] = jnp.zeros((32, 256), BF16)


def grad_one_kernel(slab, part, below, above, slope, volume, *refs):
    outs, (result, fixed) = refs[:4], refs[4:]
    fixed[:, 0:32, :] = jnp.zeros((2, 32, 256), BF16)
    fixed[:, 1056:1088, :] = jnp.zeros((2, 32, 256), BF16)
    fixed[:, 32:1056, :] = volume[...]
    hidden, outside = completed(slab[0], part, below, above)
    hidden = hidden.astype(BF16).astype(F32)
    first = jnp.where(outside, 0.0, hidden * slope[...]).astype(BF16).astype(F32)

    def store(tap_d, tap_h, tap_w, value):
        result[((2 - tap_d) * 3 + 2 - tap_h) * 3 + 2 - tap_w] = value.astype(BF16)

    tap_products(first, fixed, store)
    result[27] = jnp.zeros((32, 256), BF16)
    for step in range(4):
        outs[step][...] = result[pl.ds((slab[0] + step) % 4 * 7, 7)]


def row_kernel(slab, *refs):
    blocks, outs, held = refs[:4], refs[4:12], refs[12]
    total = blocks[0][...].astype(F32)
    for block in blocks[1:]:
        total = total + block[...].astype(F32)
    held[0:7] = total.astype(BF16)
    held[7] = jnp.zeros((32, 256), BF16)
    for step in range(8):
        outs[step][...] = held[(slab[0] // 4 + step) % 8]


def column_kernel(*refs):
    blocks, copies = refs[:8], refs[8]
    total = blocks[0][...].astype(F32)
    for block in blocks[1:]:
        total = total + block[...].astype(F32)
    total = total.astype(BF16)
    for target in range(32):
        copies[target] = total


def sum_kernel(pieces, copies):
    total = pieces[0].astype(F32)
    for source in range(1, 32):
        total = total + pieces[source].astype(F32)
    total = total.astype(BF16)
    for target in range(32):
        copies[target] = total


def pick_kernel(gathered, after, whole):
    del after
    for tap in range(27):
        whole[tap] = gathered[tap % 7 * 4 + tap // 7]


def join_kernel(place, *refs):
    chip, core = place[0] // 2, place[0] % 2
    whole, mark = refs[8:]
    mark[...] = jnp.zeros_like(mark)
    for step in range(4):
        row = (chip + 4 - step) % 4 * 64
        for block, side in ((refs[step], core), (refs[4 + step], 1 - core)):
            start = pl.multiple_of(row + side * 32, 32)
            whole[:, pl.ds(start, 32), :] = block[...]


def join(place, blocks):
    piece = pl.BlockSpec((9, 32, 256), lambda step: (step, 0, 0))
    return pl.pallas_call(
        join_kernel,
        grid=(3,),
        cost_estimate=pl.CostEstimate(flops=3 * 10**9, bytes_accessed=0, transcendentals=0),
        out_shape=[shape((27, 256, 256), BF16), shape((8, 128), F32)],
        in_specs=[SMEM] + [piece] * 8,
        out_specs=[
            pl.BlockSpec((9, 256, 256), lambda step: (step, 0, 0)),
            pl.BlockSpec((8, 128), lambda step: (0, 0)),
        ],
        compiler_params=PARAMS,
    )(place, *blocks)


def shape(dims, dtype):
    return jax.ShapeDtypeStruct(dims, dtype)


def call(kernel, in_specs, outs, scratch, *operands, cost=None):
    return pl.pallas_call(
        kernel,
        cost_estimate=cost and pl.CostEstimate(flops=cost, bytes_accessed=0, transcendentals=0),
        out_shape=outs,
        in_specs=in_specs,
        out_specs=[VMEM] * len(outs),
        scratch_shapes=scratch,
        compiler_params=PARAMS,
    )(*operands)


def neighbours(up, down):
    count = lax.axis_size("space")
    forward = [(i, i + 1) for i in range(count - 1)]
    backward = [(i + 1, i) for i in range(count - 1)]
    return lax.ppermute(up, "space", forward), lax.ppermute(down, "space", backward)


def along_y(block, step):
    pairs = [(i, i // 4 * 4 + (i + step) % 4) for i in range(32)]
    return lax.ppermute(block, "space", pairs)


def along_z(block, step):
    pairs = [(i, (i + 4 * step) % 32) for i in range(32)]
    return lax.ppermute(block, "space", pairs)


def swapped(block):
    return lax.ppermute(block, "filt", [(i, i ^ 1) for i in range(8)])


def along_chips(block):
    shifts = [[(i, (i + 2 * step) % 8) for i in range(8)] for step in (1, 2, 3)]
    return [block] + [lax.ppermute(block, "filt", shift) for shift in shifts]


def body(volume, first_weight, second_weight, cotangent):
    slab = lax.axis_index("space").astype(jnp.int32).reshape(1)
    place = lax.axis_index("filt").astype(jnp.int32)
    vol = volume.reshape(2, 1024, 256)
    weight_one = jnp.transpose(first_weight, (0, 1, 2, 4, 3)).reshape(864, 256)
    weight_two = second_weight.reshape(27, 256, 256)
    own_two = lax.dynamic_slice_in_dim(weight_two, place * 32, 32, axis=1)
    taps = (32, 32, 256)
    sent = [shape((1024, 128), F32)] + [shape((512, 128), BF16)] * 2
    spread_scratch = [pltpu.VMEM((1152, 256), BF16), pltpu.VMEM((4, 1088, 128), F32)]

    part, up, down = call(
        conv_one_kernel, [VMEM] * 2, sent, spread_scratch, vol, weight_one
    )
    below, above = neighbours(up, down)
    act, slope, blocks = call(
        activate_kernel,
        [SMEM] + [VMEM] * 3,
        [shape((1024, 128), BF16), shape((1024, 128), F32), shape((8, 192, 128), BF16)],
        [],
        slab,
        part,
        below,
        above,
    )
    blocks = lax.all_to_all(blocks, "filt", 0, 0)
    output, second_grad = call(
        conv_two_kernel,
        [VMEM] * 3,
        [shape((256, 256), BF16)] * 2,
        [pltpu.VMEM((4, 192, 256), BF16), pltpu.VMEM((3, 272, 256), F32)],
        blocks,
        weight_two,
        cotangent.reshape(256, 256),
    )
    mine = jnp.stack(along_chips(second_grad))
    other = swapped(mine)
    part, up, down, taps_two = call(
        back_kernel,
        [SMEM] + [VMEM] * 4,
        sent + [shape(taps, BF16)],
        [pltpu.VMEM((2, 1088, 256), BF16)] + spread_scratch,
        place.reshape(1),
        act,
        mine,
        other,
        own_two,
    )
    below, above = neighbours(up, down)
    pieces = lax.all_to_all(taps_two, "space", 0, 0)
    sevens = call(
        grad_one_kernel,
        [SMEM] + [VMEM] * 5,
        [shape((7, 32, 256), BF16)] * 4,
        [pltpu.VMEM((28, 32, 256), BF16), pltpu.VMEM((2, 1088, 256), BF16)],
        slab,
        part,
        below,
        above,
        slope,
        vol,
        cost=2 * 10**10,
    )
    sevens = [sevens[0]] + [along_y(sevens[step], step) for step in (1, 2, 3)]
    ones = call(
        row_kernel,
        [SMEM] + [VMEM] * 4,
        [shape((32, 256), BF16)] * 8,
        [pltpu.VMEM((8, 32, 256), BF16)],
        slab,
        *sevens,
    )
    ones = [ones[0]] + [along_z(ones[step], step) for step in range(1, 8)]
    (copies_two,) = call(sum_kernel, [VMEM], [shape(taps, BF16)], [], pieces)
    own_grad_two = lax.all_to_all(copies_two, "space", 0, 0)[:27]
    (copies_one,) = call(column_kernel, [VMEM] * 8, [shape(taps, BF16)], [], *ones, cost=2 * 10**10)
    chips = along_chips(own_grad_two)
    grad_two, joined = join(place.reshape(1), chips + [swapped(block) for block in chips])
    gathered = lax.all_to_all(copies_one, "space", 0, 0)
    (own_grad_one,) = call(
        pick_kernel,
        [VMEM, pl.BlockSpec(memory_space=pl.ANY)],
        [shape((27, 32, 256), BF16)],
        [],
        gathered,
        joined,
    )
    grad_one = jnp.transpose(own_grad_one.reshape(3, 3, 3, 32, 256), (0, 1, 2, 4, 3))
    return (
        output.reshape(2, 4, 32, 256),
        grad_one,
        grad_two.reshape(3, 3, 3, 256, 256),
    )


def solution(mesh):
    in_specs = (
        P("space", None, None, None),
        P(None, None, None, None, "filt"),
        P(),
        P("space", "filt", None, None),
    )
    out_specs = (P("space", "filt", None, None), P(None, None, None, None, "filt"), P())
    return jax.shard_map(body, mesh=mesh, in_specs=in_specs, out_specs=out_specs, check_vma=False)
```

```python
import jax
import jax.numpy as jnp
from jax import lax
from jax.experimental import pallas as pl
from jax.experimental.pallas import tpu as pltpu
from jax.sharding import PartitionSpec as P

F32 = jnp.float32
BF16 = jnp.bfloat16
PARAMS = pltpu.CompilerParams(vmem_limit_bytes=20 * 2**20)
VMEM = pl.BlockSpec(memory_space=pltpu.VMEM)
SMEM = pl.BlockSpec(memory_space=pltpu.SMEM)


def lanes(rows):
    return lax.broadcasted_iota(jnp.int32, (rows, 128), 1)


def columns(rows, width=128):
    return lax.broadcasted_iota(jnp.int32, (rows, width), 0) % 32


def spread_taps(planes, wide, acc, part, up, down):
    acc[...] = jnp.zeros_like(acc)
    for plane in range(2):
        for first in range(0, 9, 2):
            count = min(2, 9 - first)
            product = lax.dot_general(
                planes(plane),
                wide[first * 128 : (first + count) * 128, :],
                (((1,), (1,)), ((), ())),
                preferred_element_type=F32,
            )
            for group in range(first, first + count):
                tap_d, tap_h = group // 3, group % 3
                target = plane + 2 - tap_d
                start = (2 - tap_h) * 32
                acc[target, start : start + 1024, :] += product[
                    :, (group - first) * 128 : (group - first + 1) * 128
                ]
    rows = 128
    lane = lanes(rows)
    column = columns(rows)
    for chunk in range(1024 // rows):
        base = 32 + chunk * rows
        whole = jnp.zeros((rows, 128), F32)
        for target in range(4):
            left = jnp.where(column == 0, 0.0, acc[target, base - 1 : base - 1 + rows, :])
            here = acc[target, base : base + rows, :]
            right = jnp.where(column == 31, 0.0, acc[target, base + 1 : base + 1 + rows, :])
            picked = jnp.where(
                lane < 32, left, jnp.where(lane < 64, here, jnp.where(lane < 96, right, 0.0))
            )
            picked = picked + pltpu.roll(picked, 32, 1)
            picked = picked + pltpu.roll(picked, 64, 1)
            whole = jnp.where(lane // 32 == target, picked, whole)
        part[chunk * rows : (chunk + 1) * rows, :] = whole
    lane = lanes(512)
    low, high = part[0:512, :], part[512:1024, :]
    up[...] = jnp.where(lane < 64, pltpu.roll(low, 64, 1), high).astype(BF16)
    down[...] = jnp.where(lane < 64, low, pltpu.roll(high, 64, 1)).astype(BF16)


def completed(slab, part, below, above):
    lane = lanes(512)
    lower, upper = below[...].astype(F32), above[...].astype(F32)
    low = part[0:512, :] + jnp.where(lane < 64, lower, pltpu.roll(upper, 64, 1))
    high = part[512:1024, :] + jnp.where(lane < 64, pltpu.roll(lower, 64, 1), upper)
    both = jnp.concatenate([low, high], axis=0)
    lane = lanes(1024)
    outside = ((slab == 0) & (lane < 32)) | ((slab == 31) & (lane >= 96))
    return both, outside


def tap_products(moving, fixed, store):
    column = columns(1024)
    blank = jnp.zeros((8, 128), F32)
    shifted = [
        jnp.where(column == 0, 0.0, jnp.concatenate([blank[:1], moving[:-1]], axis=0)),
        moving,
        jnp.where(column == 31, 0.0, jnp.concatenate([moving[1:], blank[:1]], axis=0)),
    ]
    rows = jnp.concatenate([jnp.transpose(one).astype(BF16) for one in shifted], axis=0)
    for tap_h in range(3):
        start = (2 - tap_h) * 32
        first = jnp.dot(rows, fixed[0, start : start + 1024, :], preferred_element_type=F32)
        second = jnp.dot(rows, fixed[1, start : start + 1024, :], preferred_element_type=F32)
        for tap_w in range(3):
            for tap_d in range(3):
                at = tap_w * 128 + tap_d * 32
                store(
                    tap_d, tap_h, tap_w, first[at : at + 32, :] + second[at + 32 : at + 64, :]
                )


def conv_one_kernel(volume, weight, part, up, down, wide, acc):
    wide[...] = jnp.zeros_like(wide)
    for group in range(9):
        wide[group * 128 : group * 128 + 96, :] = weight[group * 96 : (group + 1) * 96, :]
    spread_taps(lambda plane: volume[plane], wide, acc, part, up, down)


def activate_kernel(slab, place, part, below, above, act, slope, *refs):
    outs, padded = refs[:4], refs[4]
    pre, outside = completed(slab[0], part, below, above)
    sigma = 1.0 / (1.0 + jnp.exp(-pre))
    value = jnp.where(outside, 0.0, pre * sigma).astype(BF16)
    act[...] = value
    slope[...] = jnp.where(outside, 0.0, sigma * (1.0 + pre * (1.0 - sigma)))
    padded[0:32, :] = jnp.zeros((32, 128), BF16)
    padded[32:1056, :] = value
    padded[1056:1088, :] = jnp.zeros((32, 128), BF16)
    for step in range(4):
        row = (place[0] // 2 + step) % 4 * 256
        for side in range(2):
            start = pl.multiple_of(row + side * 128, 128)
            outs[step][side] = padded[pl.ds(start, 192), :]


def conv_two_kernel(place, weight, cotangent, *refs):
    output, grad, field, acc, blocks = refs[8:]
    chip, core = place[0] // 2, place[0] % 2
    for step in range(4):
        row = (chip + 4 - step) % 4 * 2
        blocks[row + core] = refs[step][core]
        blocks[row + 1 - core] = refs[4 + step][core]
    for plane in range(4):
        field[plane] = jnp.concatenate(
            [blocks[source][:, plane * 32 : (plane + 1) * 32] for source in range(8)], axis=1
        )
    for tap_w in range(3):
        total = None
        for tap_d in range(3):
            for tap_h in range(3):
                window = jnp.concatenate(
                    [
                        field[tap_d, tap_h * 32 : tap_h * 32 + 128, :],
                        field[tap_d + 1, tap_h * 32 : tap_h * 32 + 128, :],
                    ],
                    axis=0,
                )
                product = jnp.dot(
                    window,
                    weight[(tap_d * 3 + tap_h) * 3 + tap_w],
                    preferred_element_type=F32,
                )
                total = product if total is None else total + product
        acc[tap_w, 8:264, :] = total
    column = columns(256, 256)
    pre = (
        jnp.where(column == 0, 0.0, acc[0, 7:263, :])
        + acc[1, 8:264, :]
        + jnp.where(column == 31, 0.0, acc[2, 9:265, :])
    )
    sigma = 1.0 / (1.0 + jnp.exp(-pre))
    output[...] = (pre * sigma).astype(BF16)
    slope = sigma * (1.0 + pre * (1.0 - sigma))
    grad[...] = (cotangent[...].astype(F32) * slope).astype(BF16)


def assemble(place, mine, other, fixed):
    fixed[:, 0:32, :] = jnp.zeros((2, 32, 256), BF16)
    fixed[:, 1056:1088, :] = jnp.zeros((2, 32, 256), BF16)
    chip, core = place // 2, place % 2
    for step in range(4):
        row = (chip + 4 - step) % 4 * 256
        for blocks, side in ((mine, core), (other, 1 - core)):
            start = pl.multiple_of(32 + row + side * 128, 32)
            for plane in range(2):
                fixed[plane, pl.ds(start, 128), :] = blocks[
                    step
                ][plane * 128 : (plane + 1) * 128, :]


def back_kernel(place, act, weight, *refs):
    part, up, down, result, fixed, wide, acc = refs[8:]
    assemble(place[0], refs[:4], refs[4:8], fixed)
    wide[...] = jnp.zeros_like(wide)
    for group in range(9):
        for tap_w in range(3):
            at = group * 128 + tap_w * 32
            wide[at : at + 32, :] = weight[(8 - group) * 3 + 2 - tap_w]
    spread_taps(lambda plane: fixed[plane, 32:1056, :], wide, acc, part, up, down)

    def store(tap_d, tap_h, tap_w, value):
        result[(tap_d * 3 + tap_h) * 3 + tap_w] = value.astype(BF16)

    tap_products(act[...].astype(F32), fixed, store)
    for spare in range(27, 32):
        result[spare] = jnp.zeros((32, 256), BF16)


def grad_one_kernel(slab, part, below, above, slope, volume, *refs):
    outs, (result, fixed) = refs[:4], refs[4:]
    fixed[:, 0:32, :] = jnp.zeros((2, 32, 256), BF16)
    fixed[:, 1056:1088, :] = jnp.zeros((2, 32, 256), BF16)
    fixed[:, 32:1056, :] = volume[...]
    hidden, outside = completed(slab[0], part, below, above)
    hidden = hidden.astype(BF16).astype(F32)
    first = jnp.where(outside, 0.0, hidden * slope[...]).astype(BF16).astype(F32)

    def store(tap_d, tap_h, tap_w, value):
        result[((2 - tap_d) * 3 + 2 - tap_h) * 3 + 2 - tap_w] = value.astype(BF16)

    tap_products(first, fixed, store)
    result[27] = jnp.zeros((32, 256), BF16)
    for step in range(4):
        outs[step][...] = result[pl.ds((slab[0] + step) % 4 * 7, 7)]


def row_kernel(slab, *refs):
    blocks, outs, held = refs[:4], refs[4:12], refs[12]
    total = blocks[0][...].astype(F32)
    for block in blocks[1:]:
        total = total + block[...].astype(F32)
    held[0:7] = total.astype(BF16)
    held[7] = jnp.zeros((32, 256), BF16)
    for step in range(8):
        outs[step][...] = held[(slab[0] // 4 + step) % 8]


def column_kernel(*refs):
    blocks, copies = refs[:8], refs[8]
    total = blocks[0][...].astype(F32)
    for block in blocks[1:]:
        total = total + block[...].astype(F32)
    total = total.astype(BF16)
    for target in range(32):
        copies[target] = total


def sum_kernel(pieces, copies):
    total = pieces[0].astype(F32)
    for source in range(1, 32):
        total = total + pieces[source].astype(F32)
    total = total.astype(BF16)
    for target in range(32):
        copies[target] = total


def pick_kernel(gathered, after, whole):
    del after
    for tap in range(27):
        whole[tap] = gathered[tap % 7 * 4 + tap // 7]


def join_kernel(place, *refs):
    chip, core = place[0] // 2, place[0] % 2
    whole, mark = refs[8:]
    mark[...] = jnp.zeros_like(mark)
    for step in range(4):
        row = (chip + 4 - step) % 4 * 64
        for block, side in ((refs[step], core), (refs[4 + step], 1 - core)):
            start = pl.multiple_of(row + side * 32, 32)
            whole[:, pl.ds(start, 32), :] = block[...]


def join(place, blocks):
    piece = pl.BlockSpec((9, 32, 256), lambda step: (step, 0, 0))
    return pl.pallas_call(
        join_kernel,
        grid=(3,),
        cost_estimate=pl.CostEstimate(flops=3 * 10**9, bytes_accessed=0, transcendentals=0),
        out_shape=[shape((27, 256, 256), BF16), shape((8, 128), F32)],
        in_specs=[SMEM] + [piece] * 8,
        out_specs=[
            pl.BlockSpec((9, 256, 256), lambda step: (step, 0, 0)),
            pl.BlockSpec((8, 128), lambda step: (0, 0)),
        ],
        compiler_params=PARAMS,
    )(place, *blocks)


def shape(dims, dtype):
    return jax.ShapeDtypeStruct(dims, dtype)


def call(kernel, in_specs, outs, scratch, *operands, cost=None):
    return pl.pallas_call(
        kernel,
        cost_estimate=cost and pl.CostEstimate(flops=cost, bytes_accessed=0, transcendentals=0),
        out_shape=outs,
        in_specs=in_specs,
        out_specs=[VMEM] * len(outs),
        scratch_shapes=scratch,
        compiler_params=PARAMS,
    )(*operands)


def neighbours(up, down):
    count = lax.axis_size("space")
    forward = [(i, i + 1) for i in range(count - 1)]
    backward = [(i + 1, i) for i in range(count - 1)]
    return lax.ppermute(up, "space", forward), lax.ppermute(down, "space", backward)


def along_y(block, step):
    pairs = [(i, i // 4 * 4 + (i + step) % 4) for i in range(32)]
    return lax.ppermute(block, "space", pairs)


def along_z(block, step):
    pairs = [(i, (i + 4 * step) % 32) for i in range(32)]
    return lax.ppermute(block, "space", pairs)


def swapped(block):
    return lax.ppermute(block, "filt", [(i, i ^ 1) for i in range(8)])


def along_chips(*blocks):
    shifts = [[(i, (i + 2 * step) % 8) for i in range(8)] for step in (1, 2, 3)]
    sent = blocks[1:] if len(blocks) > 1 else blocks * 3
    return [blocks[0]] + [
        lax.ppermute(block, "filt", shift) for block, shift in zip(sent, shifts)
    ]


def body(volume, first_weight, second_weight, cotangent):
    slab = lax.axis_index("space").astype(jnp.int32).reshape(1)
    place = lax.axis_index("filt").astype(jnp.int32)
    vol = volume.reshape(2, 1024, 256)
    weight_one = jnp.transpose(first_weight, (0, 1, 2, 4, 3)).reshape(864, 256)
    weight_two = second_weight.reshape(27, 256, 256)
    own_two = lax.dynamic_slice_in_dim(weight_two, place * 32, 32, axis=1)
    taps = (32, 32, 256)
    sent = [shape((1024, 128), F32)] + [shape((512, 128), BF16)] * 2
    spread_scratch = [pltpu.VMEM((1152, 256), BF16), pltpu.VMEM((4, 1088, 128), F32)]

    part, up, down = call(
        conv_one_kernel, [VMEM] * 2, sent, spread_scratch, vol, weight_one
    )
    below, above = neighbours(up, down)
    act, slope, *blocks = call(
        activate_kernel,
        [SMEM] * 2 + [VMEM] * 3,
        [shape((1024, 128), BF16), shape((1024, 128), F32)] + [shape((2, 192, 128), BF16)] * 4,
        [pltpu.VMEM((1088, 128), BF16)],
        slab,
        place.reshape(1),
        part,
        below,
        above,
    )
    blocks = along_chips(*blocks)
    output, second_grad = call(
        conv_two_kernel,
        [SMEM] + [VMEM] * 10,
        [shape((256, 256), BF16)] * 2,
        [
            pltpu.VMEM((4, 192, 256), BF16),
            pltpu.VMEM((3, 272, 256), F32),
            pltpu.VMEM((8, 192, 128), BF16),
        ],
        place.reshape(1),
        weight_two,
        cotangent.reshape(256, 256),
        *blocks,
        *[swapped(block) for block in blocks],
    )
    grads = along_chips(second_grad)
    part, up, down, taps_two = call(
        back_kernel,
        [SMEM] + [VMEM] * 10,
        sent + [shape(taps, BF16)],
        [pltpu.VMEM((2, 1088, 256), BF16)] + spread_scratch,
        place.reshape(1),
        act,
        own_two,
        *grads,
        *[swapped(block) for block in grads],
    )
    below, above = neighbours(up, down)
    pieces = lax.all_to_all(taps_two, "space", 0, 0)
    sevens = call(
        grad_one_kernel,
        [SMEM] + [VMEM] * 5,
        [shape((7, 32, 256), BF16)] * 4,
        [pltpu.VMEM((28, 32, 256), BF16), pltpu.VMEM((2, 1088, 256), BF16)],
        slab,
        part,
        below,
        above,
        slope,
        vol,
        cost=2 * 10**10,
    )
    sevens = [sevens[0]] + [along_y(sevens[step], step) for step in (1, 2, 3)]
    ones = call(
        row_kernel,
        [SMEM] + [VMEM] * 4,
        [shape((32, 256), BF16)] * 8,
        [pltpu.VMEM((8, 32, 256), BF16)],
        slab,
        *sevens,
    )
    ones = [ones[0]] + [along_z(ones[step], step) for step in range(1, 8)]
    (copies_two,) = call(sum_kernel, [VMEM], [shape(taps, BF16)], [], pieces)
    own_grad_two = lax.all_to_all(copies_two, "space", 0, 0)[:27]
    (copies_one,) = call(column_kernel, [VMEM] * 8, [shape(taps, BF16)], [], *ones, cost=2 * 10**10)
    chips = along_chips(own_grad_two)
    grad_two, joined = join(place.reshape(1), chips + [swapped(block) for block in chips])
    gathered = lax.all_to_all(copies_one, "space", 0, 0)
    (own_grad_one,) = call(
        pick_kernel,
        [VMEM, pl.BlockSpec(memory_space=pl.ANY)],
        [shape((27, 32, 256), BF16)],
        [],
        gathered,
        joined,
    )
    grad_one = jnp.transpose(own_grad_one.reshape(3, 3, 3, 32, 256), (0, 1, 2, 4, 3))
    return (
        output.reshape(2, 4, 32, 256),
        grad_one,
        grad_two.reshape(3, 3, 3, 256, 256),
    )


def solution(mesh):
    in_specs = (
        P("space", None, None, None),
        P(None, None, None, None, "filt"),
        P(),
        P("space", "filt", None, None),
    )
    out_specs = (P("space", "filt", None, None), P(None, None, None, None, "filt"), P())
    return jax.shard_map(body, mesh=mesh, in_specs=in_specs, out_specs=out_specs, check_vma=False)
```

```python
import jax
import jax.numpy as jnp
from jax import lax
from jax.experimental import pallas as pl
from jax.experimental.pallas import tpu as pltpu
from jax.sharding import PartitionSpec as P

F32 = jnp.float32
BF16 = jnp.bfloat16
PARAMS = pltpu.CompilerParams(vmem_limit_bytes=20 * 2**20)
VMEM = pl.BlockSpec(memory_space=pltpu.VMEM)
SMEM = pl.BlockSpec(memory_space=pltpu.SMEM)


def lanes(rows):
    return lax.broadcasted_iota(jnp.int32, (rows, 128), 1)


def columns(rows, width=128):
    return lax.broadcasted_iota(jnp.int32, (rows, width), 0) % 32


def spread_taps(planes, wide, acc, part, up, down):
    acc[...] = jnp.zeros_like(acc)
    for plane in range(2):
        for first in range(0, 9, 2):
            count = min(2, 9 - first)
            product = lax.dot_general(
                planes(plane),
                wide[first * 128 : (first + count) * 128, :],
                (((1,), (1,)), ((), ())),
                preferred_element_type=F32,
            )
            for group in range(first, first + count):
                tap_d, tap_h = group // 3, group % 3
                target = plane + 2 - tap_d
                start = (2 - tap_h) * 32
                acc[target, start : start + 1024, :] += product[
                    :, (group - first) * 128 : (group - first + 1) * 128
                ]
    rows = 128
    lane = lanes(rows)
    column = columns(rows)
    for chunk in range(1024 // rows):
        base = 32 + chunk * rows
        whole = jnp.zeros((rows, 128), F32)
        for target in range(4):
            left = jnp.where(column == 0, 0.0, acc[target, base - 1 : base - 1 + rows, :])
            here = acc[target, base : base + rows, :]
            right = jnp.where(column == 31, 0.0, acc[target, base + 1 : base + 1 + rows, :])
            picked = jnp.where(
                lane < 32, left, jnp.where(lane < 64, here, jnp.where(lane < 96, right, 0.0))
            )
            picked = picked + pltpu.roll(picked, 32, 1)
            picked = picked + pltpu.roll(picked, 64, 1)
            whole = jnp.where(lane // 32 == target, picked, whole)
        part[chunk * rows : (chunk + 1) * rows, :] = whole
    lane = lanes(512)
    low, high = part[0:512, :], part[512:1024, :]
    up[...] = jnp.where(lane < 64, pltpu.roll(low, 64, 1), high).astype(BF16)
    down[...] = jnp.where(lane < 64, low, pltpu.roll(high, 64, 1)).astype(BF16)


def completed(slab, part, below, above):
    lane = lanes(512)
    lower, upper = below[...].astype(F32), above[...].astype(F32)
    low = part[0:512, :] + jnp.where(lane < 64, lower, pltpu.roll(upper, 64, 1))
    high = part[512:1024, :] + jnp.where(lane < 64, pltpu.roll(lower, 64, 1), upper)
    both = jnp.concatenate([low, high], axis=0)
    lane = lanes(1024)
    outside = ((slab == 0) & (lane < 32)) | ((slab == 31) & (lane >= 96))
    return both, outside


def tap_products(moving, fixed, store):
    column = columns(1024)
    blank = jnp.zeros((8, 128), F32)
    shifted = [
        jnp.where(column == 0, 0.0, jnp.concatenate([blank[:1], moving[:-1]], axis=0)),
        moving,
        jnp.where(column == 31, 0.0, jnp.concatenate([moving[1:], blank[:1]], axis=0)),
    ]
    rows = jnp.concatenate([jnp.transpose(one).astype(BF16) for one in shifted], axis=0)
    for tap_h in range(3):
        start = (2 - tap_h) * 32
        first = jnp.dot(rows, fixed[0, start : start + 1024, :], preferred_element_type=F32)
        second = jnp.dot(rows, fixed[1, start : start + 1024, :], preferred_element_type=F32)
        for tap_w in range(3):
            for tap_d in range(3):
                at = tap_w * 128 + tap_d * 32
                store(
                    tap_d, tap_h, tap_w, first[at : at + 32, :] + second[at + 32 : at + 64, :]
                )


def conv_one_kernel(volume, weight, part, up, down, wide, acc):
    wide[...] = jnp.zeros_like(wide)
    for group in range(9):
        wide[group * 128 : group * 128 + 96, :] = weight[group * 96 : (group + 1) * 96, :]
    spread_taps(lambda plane: volume[plane], wide, acc, part, up, down)


def activate_kernel(slab, place, part, below, above, act, slope, *refs):
    outs, padded = refs[:4], refs[4]
    pre, outside = completed(slab[0], part, below, above)
    sigma = 1.0 / (1.0 + jnp.exp(-pre))
    value = jnp.where(outside, 0.0, pre * sigma).astype(BF16)
    act[...] = value
    slope[...] = jnp.where(outside, 0.0, sigma * (1.0 + pre * (1.0 - sigma)))
    padded[0:32, :] = jnp.zeros((32, 128), BF16)
    padded[32:1056, :] = value
    padded[1056:1088, :] = jnp.zeros((32, 128), BF16)
    for step in range(4):
        row = (place[0] // 2 + step) % 4 * 256
        for side in range(2):
            start = pl.multiple_of(row + side * 128, 128)
            outs[step][side] = padded[pl.ds(start, 192), :]


def conv_two_kernel(place, weight, cotangent, *refs):
    output, grad, field, acc, blocks = refs[8:]
    chip, core = place[0] // 2, place[0] % 2
    for step in range(4):
        row = (chip + 4 - step) % 4 * 2
        blocks[row + core] = refs[step][core]
        blocks[row + 1 - core] = refs[4 + step][core]
    for plane in range(4):
        field[plane] = jnp.concatenate(
            [blocks[source][:, plane * 32 : (plane + 1) * 32] for source in range(8)], axis=1
        )
    for tap_w in range(3):
        total = None
        for tap_d in range(3):
            for tap_h in range(3):
                window = jnp.concatenate(
                    [
                        field[tap_d, tap_h * 32 : tap_h * 32 + 128, :],
                        field[tap_d + 1, tap_h * 32 : tap_h * 32 + 128, :],
                    ],
                    axis=0,
                )
                product = jnp.dot(
                    window,
                    weight[(tap_d * 3 + tap_h) * 3 + tap_w],
                    preferred_element_type=F32,
                )
                total = product if total is None else total + product
        acc[tap_w, 8:264, :] = total
    column = columns(256, 256)
    pre = (
        jnp.where(column == 0, 0.0, acc[0, 7:263, :])
        + acc[1, 8:264, :]
        + jnp.where(column == 31, 0.0, acc[2, 9:265, :])
    )
    sigma = 1.0 / (1.0 + jnp.exp(-pre))
    output[...] = (pre * sigma).astype(BF16)
    slope = sigma * (1.0 + pre * (1.0 - sigma))
    grad[...] = (cotangent[...].astype(F32) * slope).astype(BF16)


def assemble(place, mine, other, fixed):
    fixed[:, 0:32, :] = jnp.zeros((2, 32, 256), BF16)
    fixed[:, 1056:1088, :] = jnp.zeros((2, 32, 256), BF16)
    chip, core = place // 2, place % 2
    for step in range(4):
        row = (chip + 4 - step) % 4 * 256
        for blocks, side in ((mine, core), (other, 1 - core)):
            start = pl.multiple_of(32 + row + side * 128, 32)
            for plane in range(2):
                fixed[plane, pl.ds(start, 128), :] = blocks[
                    step
                ][plane * 128 : (plane + 1) * 128, :]


def back_kernel(place, act, weight, *refs):
    part, up, down, result, fixed, wide, acc = refs[8:]
    assemble(place[0], refs[:4], refs[4:8], fixed)
    wide[...] = jnp.zeros_like(wide)
    for group in range(9):
        for tap_w in range(3):
            at = group * 128 + tap_w * 32
            wide[at : at + 32, :] = weight[(8 - group) * 3 + 2 - tap_w]
    spread_taps(lambda plane: fixed[plane, 32:1056, :], wide, acc, part, up, down)

    def store(tap_d, tap_h, tap_w, value):
        result[(tap_d * 3 + tap_h) * 3 + tap_w] = value.astype(BF16)

    tap_products(act[...].astype(F32), fixed, store)
    for spare in range(27, 32):
        result[spare] = jnp.zeros((32, 256), BF16)


def grad_one_kernel(slab, part, below, above, slope, volume, *refs):
    outs, (result, fixed) = refs[:4], refs[4:]
    fixed[:, 0:32, :] = jnp.zeros((2, 32, 256), BF16)
    fixed[:, 1056:1088, :] = jnp.zeros((2, 32, 256), BF16)
    fixed[:, 32:1056, :] = volume[...]
    hidden, outside = completed(slab[0], part, below, above)
    hidden = hidden.astype(BF16).astype(F32)
    first = jnp.where(outside, 0.0, hidden * slope[...]).astype(BF16).astype(F32)

    def store(tap_d, tap_h, tap_w, value):
        result[((2 - tap_d) * 3 + 2 - tap_h) * 3 + 2 - tap_w] = value.astype(BF16)

    tap_products(first, fixed, store)
    result[27] = jnp.zeros((32, 256), BF16)
    for step in range(4):
        outs[step][...] = result[pl.ds((slab[0] + step) % 4 * 7, 7)]


def row_kernel(slab, *refs):
    blocks, outs, held = refs[:4], refs[4:12], refs[12]
    total = blocks[0][...].astype(F32)
    for block in blocks[1:]:
        total = total + block[...].astype(F32)
    held[0:7] = total.astype(BF16)
    held[7] = jnp.zeros((32, 256), BF16)
    for step in range(8):
        outs[step][...] = held[(slab[0] // 4 + step) % 8]


def column_kernel(*refs):
    blocks, copies = refs[:8], refs[8]
    total = blocks[0][...].astype(F32)
    for block in blocks[1:]:
        total = total + block[...].astype(F32)
    total = total.astype(BF16)
    for target in range(32):
        copies[target] = total


def sum_kernel(pieces, copies):
    total = pieces[0].astype(F32)
    for source in range(1, 32):
        total = total + pieces[source].astype(F32)
    total = total.astype(BF16)
    for target in range(32):
        copies[target] = total


def pick_kernel(gathered, after, whole):
    del after
    for tap in range(27):
        whole[tap] = gathered[tap % 7 * 4 + tap // 7]


def join_kernel(place, *refs):
    chip, core = place[0] // 2, place[0] % 2
    whole, mark = refs[8:]
    mark[...] = jnp.zeros_like(mark)
    for step in range(4):
        row = (chip + 4 - step) % 4 * 64
        for block, side in ((refs[step], core), (refs[4 + step], 1 - core)):
            start = pl.multiple_of(row + side * 32, 32)
            whole[:, pl.ds(start, 32), :] = block[...]


def join(place, blocks):
    piece = pl.BlockSpec((3, 32, 256), lambda step: (step, 0, 0))
    return pl.pallas_call(
        join_kernel,
        grid=(9,),
        cost_estimate=pl.CostEstimate(flops=3 * 10**9, bytes_accessed=0, transcendentals=0),
        out_shape=[shape((27, 256, 256), BF16), shape((8, 128), F32)],
        in_specs=[SMEM] + [piece] * 8,
        out_specs=[
            pl.BlockSpec((3, 256, 256), lambda step: (step, 0, 0)),
            pl.BlockSpec((8, 128), lambda step: (0, 0)),
        ],
        compiler_params=PARAMS,
    )(place, *blocks)


def shape(dims, dtype):
    return jax.ShapeDtypeStruct(dims, dtype)


def call(kernel, in_specs, outs, scratch, *operands, cost=None):
    return pl.pallas_call(
        kernel,
        cost_estimate=cost and pl.CostEstimate(flops=cost, bytes_accessed=0, transcendentals=0),
        out_shape=outs,
        in_specs=in_specs,
        out_specs=[VMEM] * len(outs),
        scratch_shapes=scratch,
        compiler_params=PARAMS,
    )(*operands)


def neighbours(up, down):
    count = lax.axis_size("space")
    forward = [(i, i + 1) for i in range(count - 1)]
    backward = [(i + 1, i) for i in range(count - 1)]
    return lax.ppermute(up, "space", forward), lax.ppermute(down, "space", backward)


def along_y(block, step):
    pairs = [(i, i // 4 * 4 + (i + step) % 4) for i in range(32)]
    return lax.ppermute(block, "space", pairs)


def along_z(block, step):
    pairs = [(i, (i + 4 * step) % 32) for i in range(32)]
    return lax.ppermute(block, "space", pairs)


def swapped(block):
    return lax.ppermute(block, "filt", [(i, i ^ 1) for i in range(8)])


def along_chips(*blocks):
    shifts = [[(i, (i + 2 * step) % 8) for i in range(8)] for step in (1, 2, 3)]
    sent = blocks[1:] if len(blocks) > 1 else blocks * 3
    return [blocks[0]] + [
        lax.ppermute(block, "filt", shift) for block, shift in zip(sent, shifts)
    ]


def body(volume, first_weight, second_weight, cotangent):
    slab = lax.axis_index("space").astype(jnp.int32).reshape(1)
    place = lax.axis_index("filt").astype(jnp.int32)
    vol = volume.reshape(2, 1024, 256)
    weight_one = jnp.transpose(first_weight, (0, 1, 2, 4, 3)).reshape(864, 256)
    weight_two = second_weight.reshape(27, 256, 256)
    own_two = lax.dynamic_slice_in_dim(weight_two, place * 32, 32, axis=1)
    taps = (32, 32, 256)
    sent = [shape((1024, 128), F32)] + [shape((512, 128), BF16)] * 2
    spread_scratch = [pltpu.VMEM((1152, 256), BF16), pltpu.VMEM((4, 1088, 128), F32)]

    part, up, down = call(
        conv_one_kernel, [VMEM] * 2, sent, spread_scratch, vol, weight_one
    )
    below, above = neighbours(up, down)
    act, slope, *blocks = call(
        activate_kernel,
        [SMEM] * 2 + [VMEM] * 3,
        [shape((1024, 128), BF16), shape((1024, 128), F32)] + [shape((2, 192, 128), BF16)] * 4,
        [pltpu.VMEM((1088, 128), BF16)],
        slab,
        place.reshape(1),
        part,
        below,
        above,
    )
    blocks = along_chips(*blocks)
    output, second_grad = call(
        conv_two_kernel,
        [SMEM] + [VMEM] * 10,
        [shape((256, 256), BF16)] * 2,
        [
            pltpu.VMEM((4, 192, 256), BF16),
            pltpu.VMEM((3, 272, 256), F32),
            pltpu.VMEM((8, 192, 128), BF16),
        ],
        place.reshape(1),
        weight_two,
        cotangent.reshape(256, 256),
        *blocks,
        *[swapped(block) for block in blocks],
    )
    grads = along_chips(second_grad)
    part, up, down, taps_two = call(
        back_kernel,
        [SMEM] + [VMEM] * 10,
        sent + [shape(taps, BF16)],
        [pltpu.VMEM((2, 1088, 256), BF16)] + spread_scratch,
        place.reshape(1),
        act,
        own_two,
        *grads,
        *[swapped(block) for block in grads],
    )
    below, above = neighbours(up, down)
    pieces = lax.all_to_all(taps_two, "space", 0, 0)
    sevens = call(
        grad_one_kernel,
        [SMEM] + [VMEM] * 5,
        [shape((7, 32, 256), BF16)] * 4,
        [pltpu.VMEM((28, 32, 256), BF16), pltpu.VMEM((2, 1088, 256), BF16)],
        slab,
        part,
        below,
        above,
        slope,
        vol,
        cost=2 * 10**10,
    )
    sevens = [sevens[0]] + [along_y(sevens[step], step) for step in (1, 2, 3)]
    ones = call(
        row_kernel,
        [SMEM] + [VMEM] * 4,
        [shape((32, 256), BF16)] * 8,
        [pltpu.VMEM((8, 32, 256), BF16)],
        slab,
        *sevens,
    )
    ones = [ones[0]] + [along_z(ones[step], step) for step in range(1, 8)]
    (copies_two,) = call(sum_kernel, [VMEM], [shape(taps, BF16)], [], pieces)
    own_grad_two = lax.all_to_all(copies_two, "space", 0, 0)[:27]
    (copies_one,) = call(column_kernel, [VMEM] * 8, [shape(taps, BF16)], [], *ones, cost=2 * 10**10)
    chips = along_chips(own_grad_two)
    grad_two, joined = join(place.reshape(1), chips + [swapped(block) for block in chips])
    gathered = lax.all_to_all(copies_one, "space", 0, 0)
    (own_grad_one,) = call(
        pick_kernel,
        [VMEM, pl.BlockSpec(memory_space=pl.ANY)],
        [shape((27, 32, 256), BF16)],
        [],
        gathered,
        joined,
    )
    grad_one = jnp.transpose(own_grad_one.reshape(3, 3, 3, 32, 256), (0, 1, 2, 4, 3))
    return (
        output.reshape(2, 4, 32, 256),
        grad_one,
        grad_two.reshape(3, 3, 3, 256, 256),
    )


def solution(mesh):
    in_specs = (
        P("space", None, None, None),
        P(None, None, None, None, "filt"),
        P(),
        P("space", "filt", None, None),
    )
    out_specs = (P("space", "filt", None, None), P(None, None, None, None, "filt"), P())
    return jax.shard_map(body, mesh=mesh, in_specs=in_specs, out_specs=out_specs, check_vma=False)
```
